32 devices in a mesh: inv: 2 (over x), src: 2 (over core), gx: 8 (over z, y).
Axes of the slice: x: 2, y: 2, z: 4, core: 2. Of those that a mesh axis runs over, the one named last changes fastest.
Arguments:
- log_cond: float32 [64, 64, 128], P('inv', ('src', 'gx')), parts along dimension 0, may hold values from -2 to 1
- e_start: float32 [2, 6, 16, 32, 128], P('src', 'inv', 'gx'), parts along dimension 1, may hold values from -6 to 6
- offsets: int32 [2, 2], replicated, may hold values from 0 to 16, as said below
- rec_cells: int32 [2, 8192], P('src', 'gx'), may hold values from 0 to 8191, as said below
- observed: float32 [2, 8, 8192], P('src', 'inv', 'gx'), parts along dimension 1, may hold values from -6 to 6
Outputs:
- model_grad: float32 [64, 64, 128], P('inv', ('src', 'gx')), parts along dimension 0
The draws below stay inside these ranges and needn't reach their ends.
There are 2 independent parts, one for each index of `inv`. The reference program is written for one: setup_inputs(seed, part) draws one part's arguments, and reference() takes and returns one part's arrays. A program takes and returns all parts, laid end to end along the dimension named above; an argument that names none is the same for every part. Nothing has to cross between parts.
Inputs may be any that keep to these rules, and one draw needn't show every extreme that they name: `offsets`: column 0 of a row is that group's first model plane along x; column 1 its first model block of 4 columns along y, at most 8. `rec_cells`: in each group, positions d * 1024 to (d + 1) * 1024 - 1 name cells of footprint planes d * 2 to (d + 1) * 2 - 1, as (x - d * 2) * 32 * 128 + y * 128 + z; cells may repeat.
All inputs are finite; a program needn't handle non-finite values.
Results may differ from the reference program's by a relative error of at most 0.00002.
Values sent between devices are 32-bit elements; how exact they have to be, the bound alone decides.
A program may use at most 64 MiB of HBM per device.

```python
import jax
import jax.numpy as jnp
from jax import lax

CX = 2
MCY = 4
FZ = 128
R_DEV = 1024
STEPS = 4
GROUPS = 2
FX = 16
YBLOCKS = 8
FY = 32
MX = 32
MY = 64
RECS = 8192


def draw_offsets(key, part):
    first_key, second_key = jax.random.split(jax.random.fold_in(key, 11))
    along_x = jax.random.randint(first_key, (GROUPS,), 0, FX + 1)
    along_y = jax.random.randint(second_key, (GROUPS,), 0, YBLOCKS + 1)
    along_x = along_x.at[GROUPS - 1].set(FX)
    along_y = along_y.at[0].set(0)
    return jnp.stack([along_x, along_y], 1).astype(jnp.int32)


def draw_rec_cells(key, part):
    base = jax.random.fold_in(key, 23)
    first_key, second_key, third_key = jax.random.split(base, 3)
    plane = jax.random.randint(first_key, (GROUPS, RECS), 0, CX)
    column = jax.random.randint(second_key, (GROUPS, RECS), 0, FY)
    depth = jax.random.randint(third_key, (GROUPS, RECS), 0, FZ)
    cells = (plane * FY + column) * FZ + depth
    cells = cells.at[0, 0].set(0)
    cells = cells.at[GROUPS - 1, RECS - 1].set(CX * FY * FZ - 1)
    return cells.astype(jnp.int32)


def shard_levels(key, extent, pieces, low, top_value):
    def one(axis_at, blocks):
        heights = jax.random.uniform(jax.random.fold_in(jax.random.fold_in(key, 6), axis_at), (blocks,), jnp.float32, low / len(pieces), top_value / len(pieces))
        return jnp.repeat(jnp.exp(heights), extent[axis_at] // blocks).reshape((-1,) + (1,) * (len(extent) - axis_at - 1))

    level = one(*pieces[0])
    for cut in pieces[1:]:
        level = level * one(*cut)
    return level


def gaussian(key, dims, spread, most, shards=(), kind=jnp.bfloat16):
    array = jax.random.normal(key, dims, jnp.float32) * spread
    if len(shards) > 0:
        array = shard_levels(key, dims, shards, -0.22, 0.18) * array
    return jnp.clip(array, min=-most, max=most).astype(kind)


def setup_inputs(seed: int = 0, part: int = 0) -> dict:
    streams_of = jax.random.split(jax.random.key(seed), 6)
    part_splits = jax.random.split(jax.random.fold_in(streams_of[5], part), 6)
    return {
        "log_cond": jnp.clip(-2.0 + 3.0 * jax.random.uniform(part_splits[0], (MX, MY, FZ), jnp.float32) ** shard_levels(part_splits[0], (MX, MY, FZ), ((1, 16),), -0.2, 0.2), -2.0, 1.0),
        "e_start": gaussian(part_splits[1], (GROUPS, 3, FX, FY, FZ), 1.0, 6.0, ((0, 2), (2, 8)), jnp.float32),
        "offsets": draw_offsets(jax.random.fold_in(streams_of[5], 71), part),
        "rec_cells": draw_rec_cells(jax.random.fold_in(streams_of[5], 71), part),
        "observed": gaussian(part_splits[4], (GROUPS, STEPS, RECS), 1.0, 6.0, ((0, 2), (2, 8)), jnp.float32),
    }


electric_step = 0.5
magnetic_step = 0.5
loss_scale = 0.25


def forward_x(values, ghost):
    return jnp.concatenate([values[1:], ghost], 0) - values


def backward_x(values, ghost):
    return values - jnp.concatenate([ghost, values[:-1]], 0)


def forward_y(values):
    return jnp.pad(values[:, 1:], ((0, 0), (0, 1), (0, 0))) - values


def backward_y(values):
    return values - jnp.pad(values[:, :-1], ((0, 0), (1, 0), (0, 0)))


def forward_z(values):
    return jnp.pad(values[:, :, 1:], ((0, 0), (0, 0), (0, 1))) - values


def backward_z(values):
    return values - jnp.pad(values[:, :, :-1], ((0, 0), (0, 0), (1, 0)))


def magnetic_update(electric, magnetic, right_ghosts):
    return (magnetic[0] - magnetic_step * (forward_y(electric[2]) - forward_z(electric[1])),
            magnetic[1] - magnetic_step * (forward_z(electric[0]) - forward_x(electric[2], right_ghosts[1])),
            magnetic[2] - magnetic_step * (forward_x(electric[1], right_ghosts[0]) - forward_y(electric[0])))


def electric_update(electric, magnetic, left_ghosts, damping, driving):
    return (damping * electric[0] + driving * (backward_y(magnetic[2]) - backward_z(magnetic[1])),
            damping * electric[1] + driving * (backward_z(magnetic[0]) - backward_x(magnetic[2], left_ghosts[1])),
            damping * electric[2] + driving * (backward_x(magnetic[1], left_ghosts[0]) - backward_y(magnetic[0])))


def reference(log_cond, e_start, offsets, rec_cells, observed):
    model_grad = jnp.zeros((MX, MY, FZ), jnp.float32)
    plane = jnp.zeros((1, FY, FZ), jnp.float32)
    ghosts = (plane, plane)
    slab_base = (jnp.arange(RECS, dtype=jnp.int32) // R_DEV) * (CX * FY * FZ)
    for group in range(GROUPS):
        start_x = offsets[group, 0].astype(jnp.int32)
        start_y = (offsets[group, 1] * MCY).astype(jnp.int32)
        zero_index = jnp.zeros((), jnp.int32)
        mfoot = lax.dynamic_slice(log_cond, (start_x, start_y, zero_index), (FX, FY, FZ))
        sigma = jnp.exp(mfoot)
        absorb = loss_scale * sigma
        damping = (1.0 - absorb) / (1.0 + absorb)
        driving = electric_step / (1.0 + absorb)
        cells = rec_cells[group].astype(jnp.int32) + slab_base
        electric = (e_start[group, 0], e_start[group, 1], e_start[group, 2])
        zero_field = jnp.zeros((FX, FY, FZ), jnp.float32)
        magnetic = (zero_field, zero_field, zero_field)
        stored = []
        traces = []
        for number in range(STEPS):
            magnetic = magnetic_update(electric, magnetic, ghosts)
            electric = electric_update(electric, magnetic, ghosts, damping, driving)
            stored.append(electric)
            traces.append(electric[0].reshape(-1)[cells])
        resid = jnp.stack(traces) - observed[group]
        adjoint_e = (zero_field, zero_field, zero_field)
        adjoint_h = (zero_field, zero_field, zero_field)
        total = zero_field
        for number in range(STEPS):
            adjoint_h = magnetic_update(adjoint_e, adjoint_h, ghosts)
            adjoint_e = electric_update(adjoint_e, adjoint_h, ghosts, damping, driving)
            injected = adjoint_e[0].reshape(-1).at[cells].add(resid[STEPS - 1 - number]).reshape(FX, FY, FZ)
            adjoint_e = (injected, adjoint_e[1], adjoint_e[2])
            paired = stored[STEPS - 1 - number]
            total = total + (adjoint_e[0] * paired[0] + adjoint_e[1] * paired[1] + adjoint_e[2] * paired[2])
        gfoot = sigma * total
        current = lax.dynamic_slice(model_grad, (start_x, start_y, zero_index), (FX, FY, FZ))
        model_grad = lax.dynamic_update_slice(model_grad, current + gfoot, (start_x, start_y, zero_index))
    return model_grad
```

```python
import functools

import jax
import jax.numpy as jnp
from jax import lax
from jax.experimental import pallas as pl
from jax.experimental.pallas import tpu as pltpu
from jax.sharding import PartitionSpec as P

STEPS = 4
ROUNDS = 2 * STEPS - 1

electric_step = 0.5
magnetic_step = 0.5
loss_scale = 0.25
MESH = pl.DeviceIdType.MESH


def next_z(values):
    depth = values.shape[2]
    lane = lax.broadcasted_iota(jnp.int32, values.shape, 2)
    return jnp.where(lane == depth - 1, 0.0, pltpu.roll(values, depth - 1, 2))


def prev_z(values):
    lane = lax.broadcasted_iota(jnp.int32, values.shape, 2)
    return jnp.where(lane == 0, 0.0, pltpu.roll(values, 1, 2))


def next_y(values):
    count = values.shape[1]
    row = lax.broadcasted_iota(jnp.int32, values.shape, 1)
    return jnp.where(row == count - 1, 0.0, pltpu.roll(values, count - 1, 1))


def prev_y(values):
    row = lax.broadcasted_iota(jnp.int32, values.shape, 1)
    return jnp.where(row == 0, 0.0, pltpu.roll(values, 1, 1))


def repeat(count, body):
    if count <= 16:
        for index in range(count):
            body(index)
    else:
        pl.loop(0, count)(body)


def kernel(
    width,
    groups,
    log_ref,
    e_ref,
    offsets_ref,
    cells_ref,
    observed_ref,
    out_ref,
    model_send,
    model_recv,
    foot,
    stored,
    sources,
    to_left,
    to_right,
    from_right,
    from_left,
    padded,
    grad_send,
    grad_recv,
    model_sems,
    grad_sems,
    left_send_sems,
    left_recv_sems,
    right_send_sems,
    right_recv_sems,
):
    group = lax.axis_index("src")
    slab = lax.axis_index("gx")
    owners = groups * width
    own = group * width + slab
    planes, columns, depth = foot.shape
    model_planes, block_cols = log_ref.shape[0], log_ref.shape[1]
    blocks = columns // block_cols
    foot_x = planes * width
    room = model_planes - foot_x
    has_left = slab > 0
    has_right = slab < width - 1

    barrier = pltpu.get_barrier_semaphore()

    def greet(index):
        other = lax.rem(own + index + 1, owners)
        pl.semaphore_signal(
            barrier,
            inc=1,
            device_id={"src": other // width, "gx": lax.rem(other, width)},
            device_id_type=MESH,
        )

    repeat(owners - 1, greet)

    for source in range(groups):
        model_send[source * foot_x : (source + 1) * foot_x] = log_ref[
            pl.ds(offsets_ref[source, 0], foot_x)
        ]
    model_recv[own] = log_ref[pl.ds(offsets_ref[group, 0] + planes * slab, planes)]
    grad_recv[:, :room] = jnp.zeros((groups, room) + log_ref.shape[1:], jnp.float32)
    grad_recv[:, room + foot_x :] = jnp.zeros((groups, room) + log_ref.shape[1:], jnp.float32)
    edge = jnp.zeros((blocks, planes, block_cols, depth), jnp.float32)
    padded[:blocks] = edge
    padded[2 * blocks :] = edge

    @pl.when(jnp.logical_not(has_left))
    def _():
        from_left[...] = jnp.zeros_like(from_left)

    @pl.when(jnp.logical_not(has_right))
    def _():
        from_right[...] = jnp.zeros_like(from_right)

    def left_copy(number):
        return pltpu.make_async_remote_copy(
            src_ref=to_left.at[number],
            dst_ref=from_right.at[number],
            send_sem=left_send_sems.at[number],
            recv_sem=left_recv_sems.at[number],
            device_id={"gx": slab - 1},
            device_id_type=MESH,
        )

    def right_copy(number):
        return pltpu.make_async_remote_copy(
            src_ref=to_right.at[number],
            dst_ref=from_left.at[number],
            send_sem=right_send_sems.at[number],
            recv_sem=right_recv_sems.at[number],
            device_id={"gx": slab + 1},
            device_id_type=MESH,
        )

    def begin(number, electric, magnetic):
        ex, ey, ez = electric
        hy = magnetic[1][planes - 1 :] if magnetic is not None else 0.0
        hz = magnetic[2][planes - 1 :] if magnetic is not None else 0.0
        last_x = ex[planes - 1 :]
        part_y = hy - magnetic_step * (next_z(last_x) - last_x)
        part_z = hz + magnetic_step * (next_y(last_x) - last_x)
        if ey is not None:
            part_y = part_y - magnetic_step * ez[planes - 1 :]
            part_z = part_z + magnetic_step * ey[planes - 1 :]
            to_left[number, 0] = ey[0]
            to_left[number, 1] = ez[0]
        to_right[number, 0] = part_y[0]
        to_right[number, 1] = part_z[0]

        def send():
            if ey is not None:

                @pl.when(has_left)
                def _():
                    left_copy(number).start()

            @pl.when(has_right)
            def _():
                right_copy(number).start()

        return (part_y, part_z), send

    def finish(number, electric, magnetic, parts, coefficients):
        ex, ey, ez = electric
        part_y, part_z = parts
        damping, driving = coefficients()
        inner = magnetic is not None
        first_x = ex[: planes - 1]
        hx = magnetic[0] if inner else 0.0
        front_y = (magnetic[1][: planes - 1] if inner else 0.0) - magnetic_step * (
            next_z(first_x) - first_x
        )
        front_z = (magnetic[2][: planes - 1] if inner else 0.0) + magnetic_step * (
            next_y(first_x) - first_x
        )
        if ey is not None:
            hx = hx - magnetic_step * ((next_y(ez) - ez) - (next_z(ey) - ey))
            front_y = front_y + magnetic_step * (ez[1:] - ez[: planes - 1])
            front_z = front_z - magnetic_step * (ey[1:] - ey[: planes - 1])

            @pl.when(has_right)
            def _():
                left_copy(number).wait_recv()

            part_y = part_y + magnetic_step * from_right[number, 1][None]
            part_z = part_z - magnetic_step * from_right[number, 0][None]
        hy = jnp.concatenate([front_y, part_y], 0)
        hz = jnp.concatenate([front_z, part_z], 0)

        @pl.when(has_left)
        def _():
            right_copy(number).wait_recv()

        ghost_y = from_left[number, 0][None]
        ghost_z = from_left[number, 1][None]
        if ey is not None:
            ghost_y = ghost_y + jnp.where(has_left, magnetic_step * ez[:1], 0.0)
            ghost_z = ghost_z - jnp.where(has_left, magnetic_step * ey[:1], 0.0)
        back_y = hy - jnp.concatenate([ghost_y, hy[: planes - 1]], 0)
        back_z = hz - jnp.concatenate([ghost_z, hz[: planes - 1]], 0)
        new_x = damping * ex + driving * ((hz - prev_y(hz)) - (hy - prev_z(hy)))
        if ey is None:
            hx = jnp.zeros_like(hy)
            new_y = driving * (-back_z)
            new_z = driving * back_y
        else:
            new_y = damping * ey + driving * ((hx - prev_z(hx)) - back_z)
            new_z = damping * ez + driving * (back_y - (hx - prev_y(hx)))
        return (new_x, new_y, new_z), (hx, hy, hz)

    def model_copy(index):
        other = lax.rem(own + index + 1, owners)
        return pltpu.make_async_remote_copy(
            src_ref=model_send.at[pl.ds(planes * other, planes)],
            dst_ref=model_recv.at[own],
            send_sem=model_sems.at[0],
            recv_sem=model_sems.at[1],
            device_id={"src": other // width, "gx": lax.rem(other, width)},
            device_id_type=MESH,
        )

    def grad_copy(index):
        other = lax.rem(own + index + 1, owners)
        return pltpu.make_async_remote_copy(
            src_ref=grad_send.at[other],
            dst_ref=grad_recv.at[group, pl.ds(room + planes * slab, planes)],
            send_sem=grad_sems.at[0],
            recv_sem=grad_sems.at[1],
            device_id={"src": other // width, "gx": lax.rem(other, width)},
            device_id_type=MESH,
        )

    electric = (e_ref[0, 0], e_ref[0, 1], e_ref[0, 2])
    magnetic = None
    parts, send = begin(0, electric, magnetic)
    pl.semaphore_wait(barrier, owners - 1)
    send()
    repeat(owners - 1, lambda index: model_copy(index).start())

    cells = cells_ref[...]
    receivers = cells.shape[1]
    row_of = lax.div(cells, depth)
    lane_of = lax.rem(cells, depth)
    lane_hot = (
        lax.broadcasted_iota(jnp.int32, (depth, receivers), 0) == lane_of
    ).astype(jnp.float32).astype(jnp.bfloat16)
    values = []
    rest = observed_ref[0]
    for _ in range(3):
        piece = rest.astype(jnp.bfloat16).astype(jnp.float32)
        rest = rest - piece
        values.append(piece)
    rows = 64

    def scatter(chunk):
        hot = lax.broadcasted_iota(jnp.int32, (rows, receivers), 0) + chunk * rows == row_of
        stack = [hot.astype(jnp.float32).astype(jnp.bfloat16)]
        for number in range(STEPS):
            for piece in values:
                stack.append(
                    jnp.where(hot, piece[number : number + 1], 0.0).astype(jnp.bfloat16)
                )
        summed = lax.dot_general(
            jnp.concatenate(stack, 0),
            lane_hot,
            (((1,), (1,)), ((), ())),
            preferred_element_type=jnp.float32,
        )
        place = pl.ds(chunk * rows, rows)
        sources[0, place] = summed[:rows]
        for number in range(STEPS):
            base = rows * (1 + 3 * number)
            sources[1 + number, place] = (
                summed[base + 2 * rows : base + 3 * rows]
                + summed[base + rows : base + 2 * rows]
                + summed[base : base + rows]
            )

    repeat(planes * columns // rows, scatter)

    my_block = offsets_ref[group, 1]

    def arrived(sems, buffer, slot):
        whole = buffer.at[pl.ds(0, owners - 1)]
        pltpu.make_async_copy(whole, whole, sems.at[slot]).wait()

    held = []

    def coefficients():
        if not held:
            arrived(model_sems, model_recv, 1)
            for block in range(blocks):
                foot[:, block * block_cols : (block + 1) * block_cols] = model_recv[
                    my_block + block
                ]
            sigma = jnp.exp(foot[...])
            absorb = loss_scale * sigma
            driving = electric_step / (1.0 + absorb)
            held.append((sigma, (1.0 - absorb) / (1.0 + absorb), driving))
        return held[0][1:]

    def source_of(number, field):
        shape = (planes, columns, depth)
        return sources[0].reshape(shape) * field - sources[number].reshape(shape)

    for number in range(STEPS):
        if number:
            parts, send = begin(number, electric, magnetic)
            send()
        electric, magnetic = finish(number, electric, magnetic, parts, coefficients)
        for part in range(3):
            stored[number, part] = electric[part]

    adjoint = (source_of(STEPS, electric[0]), None, None)
    magnetic = None
    total = adjoint[0] * electric[0]
    for number in range(1, STEPS):
        turn = STEPS + number - 1
        paired = STEPS - 1 - number
        parts, send = begin(turn, adjoint, magnetic)
        send()
        adjoint, magnetic = finish(turn, adjoint, magnetic, parts, coefficients)
        adjoint = (adjoint[0] + source_of(paired + 1, stored[paired, 0]),) + adjoint[1:]
        total = total + (
            adjoint[0] * stored[paired, 0]
            + adjoint[1] * stored[paired, 1]
            + adjoint[2] * stored[paired, 2]
        )

    foot[...] = held[0][0] * total
    for block in range(blocks):
        padded[blocks + block] = foot[:, block * block_cols : (block + 1) * block_cols]
    grad_send[...] = padded[pl.ds(blocks - my_block, owners)]
    repeat(owners - 1, lambda index: grad_copy(index).start())
    grad_recv[group, pl.ds(room + planes * slab, planes)] = grad_send[own]

    arrived(model_sems, model_recv, 0)
    for number in range(ROUNDS):
        if number != STEPS:

            @pl.when(has_left)
            def _():
                left_copy(number).wait_send()

        @pl.when(has_right)
        def _():
            right_copy(number).wait_send()

    arrived(grad_sems, grad_send, 0)
    arrived(grad_sems, grad_send, 1)
    result = grad_recv[0, pl.ds(room - offsets_ref[0, 0], model_planes)]
    for source in range(1, groups):
        result = result + grad_recv[source, pl.ds(room - offsets_ref[source, 0], model_planes)]
    out_ref[...] = result


def local(log_cond, e_start, offsets, rec_cells, observed):
    groups = offsets.shape[0]
    width = lax.axis_size("gx")
    owners = groups * width
    planes, columns, depth = e_start.shape[2:]
    model_planes, block_cols = log_cond.shape[:2]
    blocks = columns // block_cols
    foot_x = planes * width
    room = model_planes - foot_x
    vmem = pl.BlockSpec(memory_space=pltpu.VMEM)
    smem = pl.BlockSpec(memory_space=pltpu.SMEM)
    piece = (planes, block_cols, depth)
    plane = (columns, depth)
    halo = pltpu.VMEM((ROUNDS, 2) + plane, jnp.float32)
    scratch = [
        pltpu.VMEM((groups * foot_x, block_cols, depth), jnp.float32),
        pltpu.VMEM((owners,) + piece, jnp.float32),
        pltpu.VMEM((planes, columns, depth), jnp.float32),
        pltpu.VMEM((STEPS, 3, planes, columns, depth), jnp.float32),
        pltpu.VMEM((STEPS + 1, planes * columns, depth), jnp.float32),
        halo,
        halo,
        halo,
        halo,
        pltpu.VMEM((3 * blocks,) + piece, jnp.float32),
        pltpu.VMEM((owners,) + piece, jnp.float32),
        pltpu.VMEM((groups, model_planes + room, block_cols, depth), jnp.float32),
        pltpu.SemaphoreType.DMA((2,)),
        pltpu.SemaphoreType.DMA((2,)),
    ] + [pltpu.SemaphoreType.DMA((ROUNDS,))] * 4
    return pl.pallas_call(
        functools.partial(kernel, width, groups),
        out_shape=jax.ShapeDtypeStruct(log_cond.shape, jnp.float32),
        in_specs=[vmem, vmem, smem, vmem, vmem],
        out_specs=vmem,
        scratch_shapes=scratch,
        compiler_params=pltpu.CompilerParams(
            collective_id=0, has_side_effects=True, vmem_limit_bytes=56 * 1024 * 1024
        ),
    )(log_cond, e_start, offsets, rec_cells, observed)


def solution(mesh):
    placed = (
        P("inv", ("src", "gx"), None),
        P("src", "inv", "gx", None, None),
        P(),
        P("src", "gx"),
        P("src", "inv", "gx"),
    )
    return jax.shard_map(
        local, mesh=mesh, in_specs=placed, out_specs=P("inv", ("src", "gx"), None), check_vma=False
    )
```

```python
import functools

import jax
import jax.numpy as jnp
from jax import lax
from jax.experimental import pallas as pl
from jax.experimental.pallas import tpu as pltpu
from jax.sharding import PartitionSpec as P

STEPS = 4

electric_step = 0.5
magnetic_step = 0.5
loss_scale = 0.25
MESH = pl.DeviceIdType.MESH


def next_z(values):
    depth = values.shape[1]
    lane = lax.broadcasted_iota(jnp.int32, values.shape, 1)
    return jnp.where(lane == depth - 1, 0.0, pltpu.roll(values, depth - 1, 1))


def prev_z(values):
    lane = lax.broadcasted_iota(jnp.int32, values.shape, 1)
    return jnp.where(lane == 0, 0.0, pltpu.roll(values, 1, 1))


def next_y(values):
    count = values.shape[0]
    row = lax.broadcasted_iota(jnp.int32, values.shape, 0)
    return jnp.where(row == count - 1, 0.0, pltpu.roll(values, count - 1, 0))


def prev_y(values):
    row = lax.broadcasted_iota(jnp.int32, values.shape, 0)
    return jnp.where(row == 0, 0.0, pltpu.roll(values, 1, 0))


def repeat(count, body):
    if count <= 16:
        for index in range(count):
            body(index)
    else:
        pl.loop(0, count)(body)


def kernel(
    width,
    groups,
    log_ref,
    e_ref,
    offsets_ref,
    cells_ref,
    observed_ref,
    out_ref,
    model_send,
    model_recv,
    foot,
    stored,
    sources,
    resid,
    far_e,
    near_foot,
    far_foot,
    left_two,
    left_resid,
    right_three,
    right_four,
    far_four,
    shaped,
    padded,
    grad_send,
    grad_recv,
    model_sems,
    grad_sems,
    send_sems,
    recv_sems,
):
    group = lax.axis_index("src")
    slab = lax.axis_index("gx")
    owners = groups * width
    own = group * width + slab
    planes, columns, depth = foot.shape
    model_planes, block_cols = log_ref.shape[0], log_ref.shape[1]
    blocks = columns // block_cols
    foot_x = planes * width
    room = model_planes - foot_x

    barrier = pltpu.get_barrier_semaphore()

    def greet(index):
        other = lax.rem(own + index + 1, owners)
        pl.semaphore_signal(
            barrier,
            inc=1,
            device_id={"src": other // width, "gx": lax.rem(other, width)},
            device_id_type=MESH,
        )

    repeat(owners - 1, greet)

    for source in range(groups):
        model_send[source * foot_x : (source + 1) * foot_x] = log_ref[
            pl.ds(offsets_ref[source, 0], foot_x)
        ]
    model_recv[own] = log_ref[pl.ds(offsets_ref[group, 0] + planes * slab, planes)]
    grad_recv[:, :room] = jnp.zeros((groups, room) + log_ref.shape[1:], jnp.float32)
    grad_recv[:, room + foot_x :] = jnp.zeros((groups, room) + log_ref.shape[1:], jnp.float32)
    edge = jnp.zeros((blocks, planes, block_cols, depth), jnp.float32)
    padded[:blocks] = edge
    padded[2 * blocks :] = edge

    def apart(steps):
        return (slab + steps >= 0) & (slab + steps < width)

    def channel(number, steps, src, dst):
        copy = pltpu.make_async_remote_copy(
            src_ref=src,
            dst_ref=dst,
            send_sem=send_sems.at[number],
            recv_sem=recv_sems.at[number],
            device_id={"gx": slab + steps},
            device_id_type=MESH,
        )

        def start():
            pl.when(apart(steps))(copy.start)

        def arrive():
            pl.when(apart(-steps))(copy.wait_recv)

        def drain():
            pl.when(apart(steps))(copy.wait_send)

        return start, arrive, drain

    sides = (-1, 1, -2, 2)
    field_ways = [channel(k, sides[k], e_ref.at[0], far_e.at[k]) for k in range(4)]
    foot_ways = [
        channel(4, -1, foot, near_foot.at[0]),
        channel(5, 1, foot, near_foot.at[1]),
        channel(6, -2, foot.at[0], far_foot.at[0]),
        channel(7, 2, foot.at[1], far_foot.at[1]),
    ]
    resid_ways = {
        2: [channel(8, 1, resid.at[0, 1], left_two)],
        3: [
            channel(9, 1, resid.at[1], left_resid.at[0]),
            channel(10, -1, resid.at[1, 0], right_three),
        ],
        4: [
            channel(11, 1, resid.at[2], left_resid.at[1]),
            channel(12, -1, resid.at[2], right_four),
            channel(13, 2, resid.at[2, 1], far_four),
        ],
    }

    @pl.when(slab < 1)
    def _():
        far_e[1] = jnp.zeros_like(far_e[1])
        near_foot[1] = jnp.zeros_like(near_foot[1])
        left_two[...] = jnp.zeros_like(left_two)
        left_resid[...] = jnp.zeros_like(left_resid)

    @pl.when(slab < 2)
    def _():
        far_e[3] = jnp.zeros_like(far_e[3])
        far_foot[1] = jnp.zeros_like(far_foot[1])
        far_four[...] = jnp.zeros_like(far_four)

    @pl.when(slab >= width - 1)
    def _():
        far_e[0] = jnp.zeros_like(far_e[0])
        near_foot[0] = jnp.zeros_like(near_foot[0])
        right_three[...] = jnp.zeros_like(right_three)
        right_four[...] = jnp.zeros_like(right_four)

    @pl.when(slab >= width - 2)
    def _():
        far_e[2] = jnp.zeros_like(far_e[2])
        far_foot[0] = jnp.zeros_like(far_foot[0])

    def inside(plane):
        place = slab * planes + plane
        return (place >= 0) & (place < foot_x)

    def advance(electric, magnetic, reach, damping, driving):
        later_h = {}
        for p in range(-reach - 1, planes + reach):
            ex, ey, ez = electric[p]
            after = electric[p + 1]
            hx, hy, hz = magnetic[p] if magnetic is not None else (0.0, 0.0, 0.0)
            step = magnetic_step if p >= 0 else jnp.where(inside(p), magnetic_step, 0.0)
            curl_y = next_z(ex) - ex
            curl_z = ex - next_y(ex)
            curl_x = None
            if ey is not None:
                curl_x = (next_y(ez) - ez) - (next_z(ey) - ey)
                curl_y = curl_y + ez
                curl_z = curl_z - ey
            if after[1] is not None:
                curl_y = curl_y - after[2]
                curl_z = curl_z + after[1]
            later_h[p] = (
                jnp.zeros_like(ex) if curl_x is None else hx - step * curl_x,
                hy - step * curl_y,
                hz - step * curl_z,
            )
        later_e = {}
        for p in range(-reach, planes + reach):
            hx, hy, hz = later_h[p]
            before = later_h[p - 1]
            ex, ey, ez = electric[p]
            new_y = driving[p] * ((hx - prev_z(hx)) - (hz - before[2]))
            new_z = driving[p] * ((hy - before[1]) - (hx - prev_y(hx)))
            new_x = driving[p] * ((hz - prev_y(hz)) - (hy - prev_z(hy)))
            if ex is not None:
                new_x = damping[p] * ex + new_x
            if ey is not None:
                new_y = damping[p] * ey + new_y
                new_z = damping[p] * ez + new_z
            later_e[p] = (new_x, new_y, new_z)
        return later_e, later_h

    def model_copy(index):
        other = lax.rem(own + index + 1, owners)
        return pltpu.make_async_remote_copy(
            src_ref=model_send.at[pl.ds(planes * other, planes)],
            dst_ref=model_recv.at[own],
            send_sem=model_sems.at[0],
            recv_sem=model_sems.at[1],
            device_id={"src": other // width, "gx": lax.rem(other, width)},
            device_id_type=MESH,
        )

    def grad_copy(index):
        other = lax.rem(own + index + 1, owners)
        return pltpu.make_async_remote_copy(
            src_ref=grad_send.at[other],
            dst_ref=grad_recv.at[group, pl.ds(room + planes * slab, planes)],
            send_sem=grad_sems.at[0],
            recv_sem=grad_sems.at[1],
            device_id={"src": other // width, "gx": lax.rem(other, width)},
            device_id_type=MESH,
        )

    pl.semaphore_wait(barrier, owners - 1)
    repeat(owners - 1, lambda index: model_copy(index).start())
    for way in field_ways:
        way[0]()

    cells = cells_ref[...]
    receivers = cells.shape[1]
    row_of = lax.div(cells, depth)
    lane_of = lax.rem(cells, depth)
    lane_hot = (
        lax.broadcasted_iota(jnp.int32, (depth, receivers), 0) == lane_of
    ).astype(jnp.float32).astype(jnp.bfloat16)
    values = []
    rest = observed_ref[0]
    for _ in range(3):
        piece = rest.astype(jnp.bfloat16).astype(jnp.float32)
        rest = rest - piece
        values.append(piece)
    rows = 64

    def scatter(chunk):
        hot = lax.broadcasted_iota(jnp.int32, (rows, receivers), 0) + chunk * rows == row_of
        stack = [hot.astype(jnp.float32).astype(jnp.bfloat16)]
        for number in range(STEPS):
            for piece in values:
                stack.append(
                    jnp.where(hot, piece[number : number + 1], 0.0).astype(jnp.bfloat16)
                )
        summed = lax.dot_general(
            jnp.concatenate(stack, 0),
            lane_hot,
            (((1,), (1,)), ((), ())),
            preferred_element_type=jnp.float32,
        )
        place = pl.ds(chunk * rows, rows)
        sources[0, place] = summed[:rows]
        for number in range(STEPS):
            base = rows * (1 + 3 * number)
            sources[1 + number, place] = (
                summed[base + 2 * rows : base + 3 * rows]
                + summed[base + rows : base + 2 * rows]
                + summed[base : base + rows]
            )

    repeat(planes * columns // rows, scatter)

    my_block = offsets_ref[group, 1]

    def arrived(sems, buffer, slot):
        whole = buffer.at[pl.ds(0, owners - 1)]
        pltpu.make_async_copy(whole, whole, sems.at[slot]).wait()

    arrived(model_sems, model_recv, 1)
    for block in range(blocks):
        foot[:, block * block_cols : (block + 1) * block_cols] = model_recv[my_block + block]
    for way in foot_ways:
        way[0]()

    damping = {}
    driving = {}
    sigma = {}

    def set_coefficients(plane, value):
        level = jnp.exp(value)
        absorb = loss_scale * level
        drive = electric_step / (1.0 + absorb)
        damp = (1.0 - absorb) / (1.0 + absorb)
        if plane < 0 or plane >= planes:
            drive = jnp.where(inside(plane), drive, 0.0)
            damp = jnp.where(inside(plane), damp, 0.0)
        sigma[plane] = level
        damping[plane] = damp
        driving[plane] = drive

    for p in range(planes):
        set_coefficients(p, foot[p])
    for way in foot_ways:
        way[1]()
    for p in range(planes):
        set_coefficients(p - planes, near_foot[1, p])
        set_coefficients(p + planes, near_foot[0, p])
    set_coefficients(-planes - 1, far_foot[1])
    set_coefficients(2 * planes, far_foot[0])
    for way in field_ways:
        way[1]()
    electric = {}
    for p in range(planes):
        electric[p] = tuple(e_ref[0, part, p] for part in range(3))
        for k in range(4):
            electric[p - sides[k] * planes] = tuple(far_e[k, part, p] for part in range(3))

    def source_of(number, plane, field):
        place = slice(plane * columns, (plane + 1) * columns)
        return sources[0, place] * field - sources[number, place]

    magnetic = None
    for number in range(1, STEPS + 1):
        electric, magnetic = advance(electric, magnetic, STEPS - number, damping, driving)
        if number > 1:
            for p in range(planes):
                resid[number - 2, p] = source_of(number, p, electric[p][0])
            for way in resid_ways[number]:
                way[0]()
        if number < STEPS:
            for p in range(planes):
                for part in range(3):
                    stored[number - 1, part, p] = electric[p][part]

    total = [resid[2, p] * electric[p][0] for p in range(planes)]
    for ways in resid_ways.values():
        for way in ways:
            way[1]()
    adjoint = {
        -3: (far_four[...], None, None),
        -2: (left_resid[1, 0], None, None),
        -1: (left_resid[1, 1], None, None),
        0: (resid[2, 0], None, None),
        1: (resid[2, 1], None, None),
        2: (right_four[0], None, None),
        3: (right_four[1], None, None),
        4: (None, None, None),
    }
    injected = {
        2: {
            -2: left_resid[0, 0],
            -1: left_resid[0, 1],
            0: resid[1, 0],
            1: resid[1, 1],
            2: right_three[...],
        },
        3: {-1: left_two[...], 0: resid[0, 0], 1: resid[0, 1]},
        4: {p: source_of(1, p, stored[0, 0, p]) for p in range(planes)},
    }
    magnetic = None
    for number in range(2, STEPS + 1):
        adjoint, magnetic = advance(adjoint, magnetic, STEPS - number, damping, driving)
        for p, value in injected[number].items():
            adjoint[p] = (adjoint[p][0] + value,) + adjoint[p][1:]
        for p in range(planes):
            for part in range(3):
                total[p] = total[p] + adjoint[p][part] * stored[STEPS - number, part, p]

    for p in range(planes):
        shaped[p] = sigma[p] * total[p]
    for block in range(blocks):
        padded[blocks + block] = shaped[:, block * block_cols : (block + 1) * block_cols]
    grad_send[...] = padded[pl.ds(blocks - my_block, owners)]
    repeat(owners - 1, lambda index: grad_copy(index).start())
    grad_recv[group, pl.ds(room + planes * slab, planes)] = grad_send[own]

    arrived(model_sems, model_recv, 0)
    for way in field_ways + foot_ways + sum(resid_ways.values(), []):
        way[2]()
    arrived(grad_sems, grad_send, 0)
    arrived(grad_sems, grad_send, 1)
    result = grad_recv[0, pl.ds(room - offsets_ref[0, 0], model_planes)]
    for source in range(1, groups):
        result = result + grad_recv[source, pl.ds(room - offsets_ref[source, 0], model_planes)]
    out_ref[...] = result


def local(log_cond, e_start, offsets, rec_cells, observed):
    groups = offsets.shape[0]
    width = lax.axis_size("gx")
    owners = groups * width
    planes, columns, depth = e_start.shape[2:]
    model_planes, block_cols = log_cond.shape[:2]
    blocks = columns // block_cols
    foot_x = planes * width
    room = model_planes - foot_x
    vmem = pl.BlockSpec(memory_space=pltpu.VMEM)
    smem = pl.BlockSpec(memory_space=pltpu.SMEM)
    piece = (planes, block_cols, depth)
    plane = (columns, depth)

    def vmem_of(*shape):
        return pltpu.VMEM(shape, jnp.float32)

    scratch = [
        pltpu.VMEM((groups * foot_x, block_cols, depth), jnp.float32),
        pltpu.VMEM((owners,) + piece, jnp.float32),
        pltpu.VMEM((planes, columns, depth), jnp.float32),
        pltpu.VMEM((STEPS - 1, 3, planes, columns, depth), jnp.float32),
        pltpu.VMEM((STEPS + 1, planes * columns, depth), jnp.float32),
        vmem_of(3, planes, *plane),
        vmem_of(4, 3, planes, *plane),
        vmem_of(2, planes, *plane),
        vmem_of(2, *plane),
        vmem_of(*plane),
        vmem_of(2, planes, *plane),
        vmem_of(*plane),
        vmem_of(planes, *plane),
        vmem_of(*plane),
        vmem_of(planes, *plane),
        pltpu.VMEM((3 * blocks,) + piece, jnp.float32),
        pltpu.VMEM((owners,) + piece, jnp.float32),
        pltpu.VMEM((groups, model_planes + room, block_cols, depth), jnp.float32),
        pltpu.SemaphoreType.DMA((2,)),
        pltpu.SemaphoreType.DMA((2,)),
        pltpu.SemaphoreType.DMA((14,)),
        pltpu.SemaphoreType.DMA((14,)),
    ]
    return pl.pallas_call(
        functools.partial(kernel, width, groups),
        out_shape=jax.ShapeDtypeStruct(log_cond.shape, jnp.float32),
        in_specs=[vmem, vmem, smem, vmem, vmem],
        out_specs=vmem,
        scratch_shapes=scratch,
        compiler_params=pltpu.CompilerParams(
            collective_id=0, has_side_effects=True, vmem_limit_bytes=56 * 1024 * 1024
        ),
    )(log_cond, e_start, offsets, rec_cells, observed)


def solution(mesh):
    placed = (
        P("inv", ("src", "gx"), None),
        P("src", "inv", "gx", None, None),
        P(),
        P("src", "gx"),
        P("src", "inv", "gx"),
    )
    return jax.shard_map(
        local, mesh=mesh, in_specs=placed, out_specs=P("inv", ("src", "gx"), None), check_vma=False
    )
```

```python
import functools

import jax
import jax.numpy as jnp
from jax import lax
from jax.experimental import pallas as pl
from jax.experimental.pallas import tpu as pltpu
from jax.sharding import PartitionSpec as P

STEPS = 4

electric_step = 0.5
magnetic_step = 0.5
loss_scale = 0.25
MESH = pl.DeviceIdType.MESH


def next_z(values):
    depth = values.shape[1]
    lane = lax.broadcasted_iota(jnp.int32, values.shape, 1)
    return jnp.where(lane == depth - 1, 0.0, pltpu.roll(values, depth - 1, 1))


def prev_z(values):
    lane = lax.broadcasted_iota(jnp.int32, values.shape, 1)
    return jnp.where(lane == 0, 0.0, pltpu.roll(values, 1, 1))


def next_y(values):
    count = values.shape[0]
    row = lax.broadcasted_iota(jnp.int32, values.shape, 0)
    return jnp.where(row == count - 1, 0.0, pltpu.roll(values, count - 1, 0))


def prev_y(values):
    row = lax.broadcasted_iota(jnp.int32, values.shape, 0)
    return jnp.where(row == 0, 0.0, pltpu.roll(values, 1, 0))


def repeat(count, body):
    if count <= 16:
        for index in range(count):
            body(index)
    else:
        pl.loop(0, count)(body)


def kernel(
    width,
    groups,
    log_in,
    e_in,
    offsets_in,
    cells_in,
    observed_in,
    out_ref,
    log_ref,
    e_ref,
    offsets_ref,
    cells_ref,
    observed_ref,
    load_sems,
    model_send,
    model_recv,
    foot,
    stored,
    sources,
    resid,
    far_e,
    near_foot,
    far_foot,
    left_two,
    left_resid,
    right_three,
    right_four,
    far_four,
    shaped,
    padded,
    grad_send,
    grad_recv,
    model_sems,
    grad_sems,
    send_sems,
    recv_sems,
):
    group = lax.axis_index("src")
    slab = lax.axis_index("gx")
    owners = groups * width
    own = group * width + slab
    planes, columns, depth = foot.shape
    model_planes, block_cols = log_ref.shape[0], log_ref.shape[1]
    blocks = columns // block_cols
    foot_x = planes * width
    room = model_planes - foot_x

    barrier = pltpu.get_barrier_semaphore()

    def greet(index):
        other = lax.rem(own + index + 1, owners)
        pl.semaphore_signal(
            barrier,
            inc=1,
            device_id={"src": other // width, "gx": lax.rem(other, width)},
            device_id_type=MESH,
        )

    repeat(owners - 1, greet)
    loads = [
        pltpu.make_async_copy(src, dst, load_sems.at[k])
        for k, (src, dst) in enumerate(
            (
                (offsets_in, offsets_ref),
                (log_in, log_ref),
                (e_in, e_ref),
                (cells_in, cells_ref),
                (observed_in, observed_ref),
            )
        )
    ]
    for load in loads:
        load.start()
    for load in loads[:3]:
        load.wait()

    for source in range(groups):
        model_send[source * foot_x : (source + 1) * foot_x] = log_ref[
            pl.ds(offsets_ref[source, 0], foot_x)
        ]
    model_recv[own] = log_ref[pl.ds(offsets_ref[group, 0] + planes * slab, planes)]
    grad_recv[:, :room] = jnp.zeros((groups, room) + log_ref.shape[1:], jnp.float32)
    grad_recv[:, room + foot_x :] = jnp.zeros((groups, room) + log_ref.shape[1:], jnp.float32)
    edge = jnp.zeros((blocks, planes, block_cols, depth), jnp.float32)
    padded[:blocks] = edge
    padded[2 * blocks :] = edge

    def apart(steps):
        return (slab + steps >= 0) & (slab + steps < width)

    def channel(number, steps, src, dst):
        copy = pltpu.make_async_remote_copy(
            src_ref=src,
            dst_ref=dst,
            send_sem=send_sems.at[number],
            recv_sem=recv_sems.at[number],
            device_id={"gx": slab + steps},
            device_id_type=MESH,
        )

        def start():
            pl.when(apart(steps))(copy.start)

        def arrive():
            pl.when(apart(-steps))(copy.wait_recv)

        def drain():
            pl.when(apart(steps))(copy.wait_send)

        return start, arrive, drain

    sides = (-1, 1, -2, 2)
    field_ways = [channel(k, sides[k], e_ref.at[0], far_e.at[k]) for k in range(4)]
    foot_ways = [
        channel(4, -1, foot, near_foot.at[0]),
        channel(5, 1, foot, near_foot.at[1]),
        channel(6, -2, foot.at[0], far_foot.at[0]),
        channel(7, 2, foot.at[1], far_foot.at[1]),
    ]
    resid_ways = {
        2: [channel(8, 1, resid.at[0, 1], left_two)],
        3: [
            channel(9, 1, resid.at[1], left_resid.at[0]),
            channel(10, -1, resid.at[1, 0], right_three),
        ],
        4: [
            channel(11, 1, resid.at[2], left_resid.at[1]),
            channel(12, -1, resid.at[2], right_four),
            channel(13, 2, resid.at[2, 1], far_four),
        ],
    }

    @pl.when(slab < 1)
    def _():
        far_e[1] = jnp.zeros_like(far_e[1])
        near_foot[1] = jnp.zeros_like(near_foot[1])
        left_two[...] = jnp.zeros_like(left_two)
        left_resid[...] = jnp.zeros_like(left_resid)

    @pl.when(slab < 2)
    def _():
        far_e[3] = jnp.zeros_like(far_e[3])
        far_foot[1] = jnp.zeros_like(far_foot[1])
        far_four[...] = jnp.zeros_like(far_four)

    @pl.when(slab >= width - 1)
    def _():
        far_e[0] = jnp.zeros_like(far_e[0])
        near_foot[0] = jnp.zeros_like(near_foot[0])
        right_three[...] = jnp.zeros_like(right_three)
        right_four[...] = jnp.zeros_like(right_four)

    @pl.when(slab >= width - 2)
    def _():
        far_e[2] = jnp.zeros_like(far_e[2])
        far_foot[0] = jnp.zeros_like(far_foot[0])

    def inside(plane):
        place = slab * planes + plane
        return (place >= 0) & (place < foot_x)

    def advance(electric, magnetic, reach, damping, driving):
        later_h = {}
        for p in range(-reach - 1, planes + reach):
            ex, ey, ez = electric[p]
            after = electric[p + 1]
            hx, hy, hz = magnetic[p] if magnetic is not None else (0.0, 0.0, 0.0)
            step = magnetic_step if p >= 0 else jnp.where(inside(p), magnetic_step, 0.0)
            curl_y = next_z(ex) - ex
            curl_z = ex - next_y(ex)
            curl_x = None
            if ey is not None:
                curl_x = (next_y(ez) - ez) - (next_z(ey) - ey)
                curl_y = curl_y + ez
                curl_z = curl_z - ey
            if after[1] is not None:
                curl_y = curl_y - after[2]
                curl_z = curl_z + after[1]
            later_h[p] = (
                jnp.zeros_like(ex) if curl_x is None else hx - step * curl_x,
                hy - step * curl_y,
                hz - step * curl_z,
            )
        later_e = {}
        for p in range(-reach, planes + reach):
            hx, hy, hz = later_h[p]
            before = later_h[p - 1]
            ex, ey, ez = electric[p]
            new_y = driving[p] * ((hx - prev_z(hx)) - (hz - before[2]))
            new_z = driving[p] * ((hy - before[1]) - (hx - prev_y(hx)))
            new_x = driving[p] * ((hz - prev_y(hz)) - (hy - prev_z(hy)))
            if ex is not None:
                new_x = damping[p] * ex + new_x
            if ey is not None:
                new_y = damping[p] * ey + new_y
                new_z = damping[p] * ez + new_z
            later_e[p] = (new_x, new_y, new_z)
        return later_e, later_h

    def model_copy(index):
        other = lax.rem(own + index + 1, owners)
        return pltpu.make_async_remote_copy(
            src_ref=model_send.at[pl.ds(planes * other, planes)],
            dst_ref=model_recv.at[own],
            send_sem=model_sems.at[0],
            recv_sem=model_sems.at[1],
            device_id={"src": other // width, "gx": lax.rem(other, width)},
            device_id_type=MESH,
        )

    def grad_copy(index):
        other = lax.rem(own + index + 1, owners)
        return pltpu.make_async_remote_copy(
            src_ref=grad_send.at[other],
            dst_ref=grad_recv.at[group, pl.ds(room + planes * slab, planes)],
            send_sem=grad_sems.at[0],
            recv_sem=grad_sems.at[1],
            device_id={"src": other // width, "gx": lax.rem(other, width)},
            device_id_type=MESH,
        )

    pl.semaphore_wait(barrier, owners - 1)
    repeat(owners - 1, lambda index: model_copy(index).start())
    for way in field_ways:
        way[0]()

    for load in loads[3:]:
        load.wait()
    cells = cells_ref[...]
    receivers = cells.shape[1]
    row_of = lax.div(cells, depth)
    lane_of = lax.rem(cells, depth)
    lane_hot = (
        lax.broadcasted_iota(jnp.int32, (depth, receivers), 0) == lane_of
    ).astype(jnp.float32).astype(jnp.bfloat16)
    values = []
    rest = observed_ref[0]
    for _ in range(3):
        piece = rest.astype(jnp.bfloat16).astype(jnp.float32)
        rest = rest - piece
        values.append(piece)
    rows = 64

    def scatter(chunk):
        hot = lax.broadcasted_iota(jnp.int32, (rows, receivers), 0) + chunk * rows == row_of
        stack = [hot.astype(jnp.float32).astype(jnp.bfloat16)]
        for number in range(STEPS):
            for piece in values:
                stack.append(
                    jnp.where(hot, piece[number : number + 1], 0.0).astype(jnp.bfloat16)
                )
        summed = lax.dot_general(
            jnp.concatenate(stack, 0),
            lane_hot,
            (((1,), (1,)), ((), ())),
            preferred_element_type=jnp.float32,
        )
        place = pl.ds(chunk * rows, rows)
        sources[0, place] = summed[:rows]
        for number in range(STEPS):
            base = rows * (1 + 3 * number)
            sources[1 + number, place] = (
                summed[base + 2 * rows : base + 3 * rows]
                + summed[base + rows : base + 2 * rows]
                + summed[base : base + rows]
            )

    repeat(planes * columns // rows, scatter)

    my_block = offsets_ref[group, 1]

    def arrived(sems, buffer, slot):
        whole = buffer.at[pl.ds(0, owners - 1)]
        pltpu.make_async_copy(whole, whole, sems.at[slot]).wait()

    arrived(model_sems, model_recv, 1)
    for block in range(blocks):
        foot[:, block * block_cols : (block + 1) * block_cols] = model_recv[my_block + block]
    for way in foot_ways:
        way[0]()

    damping = {}
    driving = {}
    sigma = {}

    def set_coefficients(plane, value):
        level = jnp.exp(value)
        absorb = loss_scale * level
        drive = electric_step / (1.0 + absorb)
        damp = (1.0 - absorb) / (1.0 + absorb)
        if plane < 0 or plane >= planes:
            drive = jnp.where(inside(plane), drive, 0.0)
            damp = jnp.where(inside(plane), damp, 0.0)
        sigma[plane] = level
        damping[plane] = damp
        driving[plane] = drive

    for p in range(planes):
        set_coefficients(p, foot[p])
    for way in foot_ways:
        way[1]()
    for p in range(planes):
        set_coefficients(p - planes, near_foot[1, p])
        set_coefficients(p + planes, near_foot[0, p])
    set_coefficients(-planes - 1, far_foot[1])
    set_coefficients(2 * planes, far_foot[0])
    for way in field_ways:
        way[1]()
    electric = {}
    for p in range(planes):
        electric[p] = tuple(e_ref[0, part, p] for part in range(3))
        for k in range(4):
            electric[p - sides[k] * planes] = tuple(far_e[k, part, p] for part in range(3))

    def source_of(number, plane, field):
        place = slice(plane * columns, (plane + 1) * columns)
        return sources[0, place] * field - sources[number, place]

    magnetic = None
    for number in range(1, STEPS + 1):
        electric, magnetic = advance(electric, magnetic, STEPS - number, damping, driving)
        if number > 1:
            for p in range(planes):
                resid[number - 2, p] = source_of(number, p, electric[p][0])
            for way in resid_ways[number]:
                way[0]()
        if number < STEPS:
            for p in range(planes):
                for part in range(3):
                    stored[number - 1, part, p] = electric[p][part]

    total = [resid[2, p] * electric[p][0] for p in range(planes)]
    for ways in resid_ways.values():
        for way in ways:
            way[1]()
    adjoint = {
        -3: (far_four[...], None, None),
        -2: (left_resid[1, 0], None, None),
        -1: (left_resid[1, 1], None, None),
        0: (resid[2, 0], None, None),
        1: (resid[2, 1], None, None),
        2: (right_four[0], None, None),
        3: (right_four[1], None, None),
        4: (None, None, None),
    }
    injected = {
        2: {
            -2: left_resid[0, 0],
            -1: left_resid[0, 1],
            0: resid[1, 0],
            1: resid[1, 1],
            2: right_three[...],
        },
        3: {-1: left_two[...], 0: resid[0, 0], 1: resid[0, 1]},
        4: {p: source_of(1, p, stored[0, 0, p]) for p in range(planes)},
    }
    magnetic = None
    for number in range(2, STEPS + 1):
        adjoint, magnetic = advance(adjoint, magnetic, STEPS - number, damping, driving)
        for p, value in injected[number].items():
            adjoint[p] = (adjoint[p][0] + value,) + adjoint[p][1:]
        for p in range(planes):
            for part in range(3):
                total[p] = total[p] + adjoint[p][part] * stored[STEPS - number, part, p]

    for p in range(planes):
        shaped[p] = sigma[p] * total[p]
    for block in range(blocks):
        padded[blocks + block] = shaped[:, block * block_cols : (block + 1) * block_cols]
    grad_send[...] = padded[pl.ds(blocks - my_block, owners)]
    repeat(owners - 1, lambda index: grad_copy(index).start())
    grad_recv[group, pl.ds(room + planes * slab, planes)] = grad_send[own]

    arrived(model_sems, model_recv, 0)
    for way in field_ways + foot_ways + sum(resid_ways.values(), []):
        way[2]()
    arrived(grad_sems, grad_send, 0)
    arrived(grad_sems, grad_send, 1)
    result = grad_recv[0, pl.ds(room - offsets_ref[0, 0], model_planes)]
    for source in range(1, groups):
        result = result + grad_recv[source, pl.ds(room - offsets_ref[source, 0], model_planes)]
    out_ref[...] = result


def local(log_cond, e_start, offsets, rec_cells, observed):
    groups = offsets.shape[0]
    width = lax.axis_size("gx")
    owners = groups * width
    planes, columns, depth = e_start.shape[2:]
    model_planes, block_cols = log_cond.shape[:2]
    blocks = columns // block_cols
    foot_x = planes * width
    room = model_planes - foot_x
    vmem = pl.BlockSpec(memory_space=pltpu.VMEM)
    piece = (planes, block_cols, depth)
    plane = (columns, depth)

    def vmem_of(*shape):
        return pltpu.VMEM(shape, jnp.float32)

    scratch = [
        pltpu.VMEM(log_cond.shape, jnp.float32),
        pltpu.VMEM(e_start.shape, jnp.float32),
        pltpu.SMEM(offsets.shape, jnp.int32),
        pltpu.VMEM(rec_cells.shape, jnp.int32),
        pltpu.VMEM(observed.shape, jnp.float32),
        pltpu.SemaphoreType.DMA((5,)),
        pltpu.VMEM((groups * foot_x, block_cols, depth), jnp.float32),
        pltpu.VMEM((owners,) + piece, jnp.float32),
        pltpu.VMEM((planes, columns, depth), jnp.float32),
        pltpu.VMEM((STEPS - 1, 3, planes, columns, depth), jnp.float32),
        pltpu.VMEM((STEPS + 1, planes * columns, depth), jnp.float32),
        vmem_of(3, planes, *plane),
        vmem_of(4, 3, planes, *plane),
        vmem_of(2, planes, *plane),
        vmem_of(2, *plane),
        vmem_of(*plane),
        vmem_of(2, planes, *plane),
        vmem_of(*plane),
        vmem_of(planes, *plane),
        vmem_of(*plane),
        vmem_of(planes, *plane),
        pltpu.VMEM((3 * blocks,) + piece, jnp.float32),
        pltpu.VMEM((owners,) + piece, jnp.float32),
        pltpu.VMEM((groups, model_planes + room, block_cols, depth), jnp.float32),
        pltpu.SemaphoreType.DMA((2,)),
        pltpu.SemaphoreType.DMA((2,)),
        pltpu.SemaphoreType.DMA((14,)),
        pltpu.SemaphoreType.DMA((14,)),
    ]
    return pl.pallas_call(
        functools.partial(kernel, width, groups),
        out_shape=jax.ShapeDtypeStruct(log_cond.shape, jnp.float32),
        in_specs=[pl.BlockSpec(memory_space=pl.ANY)] * 5,
        out_specs=vmem,
        scratch_shapes=scratch,
        compiler_params=pltpu.CompilerParams(
            collective_id=0, has_side_effects=True, vmem_limit_bytes=56 * 1024 * 1024
        ),
    )(log_cond, e_start, offsets, rec_cells, observed)


def solution(mesh):
    placed = (
        P("inv", ("src", "gx"), None),
        P("src", "inv", "gx", None, None),
        P(),
        P("src", "gx"),
        P("src", "inv", "gx"),
    )
    return jax.shard_map(
        local, mesh=mesh, in_specs=placed, out_specs=P("inv", ("src", "gx"), None), check_vma=False
    )
```
